256 devices in a mesh: elem: 64 (over z, y, core), lev: 4 (over x).
Axes of the slice: x: 4, y: 4, z: 8, core: 2. Of those that a mesh axis runs over, the one named last changes fastest.
Arguments:
- winds: float32 [2, 8, 16, 16384], P(None, 'lev', None, 'elem'), may hold values from -6 to 6
- surface: float32 [16, 16384], P(None, 'elem'), may hold values from -6 to 6
- thickness: float32 [8], P('lev'), may hold values from 0.05 to 0.5
- tracers: float32 [8, 9, 16384, 224], P('lev', None, 'elem'), may hold values from 0.1 to 10
- neighbours: int32 [4, 16384], P(None, 'elem'), may hold values from 0 to 16383, as said below
- rotations: int32 [4, 16384], P(None, 'elem'), may hold values from 4 to 7, as said below
- live_count: int32 [64], P('elem'), may hold values from 128 to 256, as said below
Outputs:
- winds_out: float32 [2, 8, 16, 16384], P(None, 'lev', None, 'elem')
- surface_out: float32 [16, 16384], P(None, 'elem')
- tracers_out: float32 [8, 9, 16384, 224], P('lev', None, 'elem')
The draws below stay inside these ranges and needn't reach their ends.
Inputs may be any that keep to these rules, and one draw needn't show every extreme that they name: `live_count`: the live slots of a device are its first ones and their number is a multiple of 16; one device has all 256 live, one has exactly half of them, each has at least half. `neighbours`: neighbours of live slots are live slots and mutual: if g is across edge k of e with code r, then e is across edge r mod 4 of g. A neighbour on another device is one of the last 16 live slots of the device before, or one of the first 16 slots of the device after, along the curve, which closes into a loop. `rotations`: codes of live slots agree with the neighbours from both sides.
All inputs are finite; a program needn't handle non-finite values.
Results may differ from the reference program's by a relative error of at most 0.0003.
Values sent between devices are 32-bit elements; how exact they have to be, the bound alone decides.
No kernel may reach another device: no remote copies, remote signals or barrier semaphores. Data moves between devices by JAX's collectives and lax.ppermute only.
A program may use at most 128 MiB of HBM per device.

```python
import math
import jax
import jax.numpy as jnp
import numpy as np
from jax import lax

E_DEV = 256
BAND = 16
NTRAC = 224
ELEMS = 16384
NLEV = 8


def mesh_layout(key):
    devices = ELEMS // E_DEV
    blocks = jax.random.randint(jax.random.fold_in(key, 11), (devices,), E_DEV // (2 * BAND), E_DEV // BAND + 1)
    places = jnp.arange(devices)
    blocks = jnp.where(places == devices - 1, E_DEV // BAND, blocks)
    blocks = jnp.where(places == 1, E_DEV // (2 * BAND), blocks)
    counts = (blocks * BAND).astype(jnp.int32)
    starts = (jnp.cumsum(counts) - counts).astype(jnp.int32)
    total = jnp.sum(counts).astype(jnp.int32)
    turns = jax.random.randint(jax.random.fold_in(key, 12), (ELEMS,), 0, 4).astype(jnp.int32)
    return (counts, starts, total, turns)


def edge_tables(key):
    counts, starts, total, turns = mesh_layout(key)
    slot_ids = jnp.arange(ELEMS, dtype=jnp.int32)
    owner = slot_ids // E_DEV
    local = slot_ids % E_DEV
    live = local < jnp.take(counts, owner)
    global_id = jnp.take(starts, owner) + local
    columns = total // BAND
    column_id = global_id // BAND % columns
    row_id = global_id % BAND
    slot_rows = []
    code_rows = []
    for facing in range(4):
        direction = (facing + turns) % 4
        row_step = jnp.where(direction == 0, -1, jnp.where(direction == 2, 1, 0))
        column_step = jnp.where(direction == 1, 1, jnp.where(direction == 3, -1, 0))
        other_row = (row_id + row_step + BAND) % BAND
        other_column = (column_id + column_step + columns) % columns
        other_id = other_column * BAND + other_row
        other_device = jnp.sum((starts[:, None] <= other_id[None, :]).astype(jnp.int32), axis=0) - 1
        other_slot = other_device * E_DEV + other_id - jnp.take(starts, other_device)
        back = (direction + 2 - jnp.take(turns, other_slot)) % 4
        slot_rows.append(jnp.where(live, other_slot, owner * E_DEV))
        code_rows.append(jnp.where(live, back + 4, 4))
    return (jnp.stack(slot_rows).astype(jnp.int32), jnp.stack(code_rows).astype(jnp.int32))


def draw_live_count(key, part):
    return mesh_layout(key)[0]


def draw_neighbours(key, part):
    return edge_tables(key)[0]


def draw_rotations(key, part):
    return edge_tables(key)[1]


def steps_of(key, extent, split, smallest, largest):
    gain = 1.0
    for axis_at, parts in split:
        steps = jax.random.uniform(jax.random.fold_in(jax.random.fold_in(key, 6), axis_at), (parts,), jnp.float32, smallest / len(split), largest / len(split))
        gain = gain * jnp.repeat(jnp.exp(steps), extent[axis_at] // parts).reshape((-1,) + (1,) * (len(extent) - 1 - axis_at))
    return gain


def normal_values(key, dims, spread, bound, shards=(), kind=jnp.bfloat16):
    gain = steps_of(key, dims, shards, -0.22, 0.18) if shards else 1.0
    values = jax.random.normal(key, dims, jnp.float32) * spread * gain
    return jnp.minimum(jnp.maximum(values, -bound), bound).astype(kind)


def setup_inputs(seed: int = 0) -> dict:
    seeds = jax.random.split(jax.random.key(seed), 8)
    return {
        "winds": normal_values(seeds[0], (2, NLEV, 16, ELEMS), 1.0, 6.0, ((1, 4), (3, 64)), jnp.float32),
        "surface": normal_values(seeds[1], (16, ELEMS), 1.0, 6.0, ((1, 64),), jnp.float32),
        "thickness": jnp.clip(jnp.exp(math.log(0.5) - 2.3025851 * jax.random.uniform(seeds[2], (NLEV,), jnp.float32) ** steps_of(seeds[2], (NLEV,), ((0, 4),), -0.2, 0.2)), 0.05, 0.5),
        "tracers": jnp.clip(jnp.exp(math.log(10.0) - 4.6051702 * jax.random.uniform(seeds[3], (NLEV, 9, ELEMS, NTRAC), jnp.float32) ** steps_of(seeds[3], (NLEV, 9, ELEMS, NTRAC), ((0, 4), (2, 64)), -0.2, 0.2)), 0.1, 10.0),
        "neighbours": draw_neighbours(jax.random.fold_in(seeds[7], 71), 0),
        "rotations": draw_rotations(jax.random.fold_in(seeds[7], 71), 0),
        "live_count": draw_live_count(jax.random.fold_in(seeds[7], 71), 0),
    }


PRECISE = lax.Precision.HIGHEST
STEP = 0.1
COURANT = 0.45
NODE_EDGES = [[0, 1, 2, 3], [3, 7, 11, 15], [15, 14, 13, 12], [12, 8, 4, 0]]
CELL_EDGES = [[0, 1, 2], [2, 5, 8], [8, 7, 6], [6, 3, 0]]
BORDER_NODES = [0, 1, 2, 3, 4, 7, 8, 11, 12, 13, 14, 15]
BORDER_CELLS = [0, 1, 2, 3, 5, 6, 7, 8]


def node_tables():
    points = np.array([-1.0, -0.2 ** 0.5, 0.2 ** 0.5, 1.0])
    products = np.array([np.prod([points[a] - points[k] for k in range(4) if k != a]) for a in range(4)])
    derivative = np.zeros((4, 4))
    for source in range(4):
        for target in range(4):
            if source != target:
                derivative[source, target] = products[source] / products[target] / (points[source] - points[target])
        derivative[source, source] = sum(1.0 / (points[source] - points[k]) for k in range(4) if k != source)
    identity = np.eye(4)
    along_x = np.kron(identity, derivative)
    along_y = np.kron(derivative, identity)
    centers = np.array([-2.0 / 3.0, 0.0, 2.0 / 3.0])
    lagrange = np.array([[np.prod([(t - points[k]) / (points[b] - points[k]) for k in range(4) if k != b]) for b in range(4)] for t in centers])
    to_cells = np.kron(lagrange, lagrange)
    scatter = np.zeros((16, 16))
    for facing in range(4):
        for station in range(4):
            scatter[NODE_EDGES[facing][station], 4 * facing + station] = 1.0
    multiplicity = 1.0 + scatter.sum(axis=1)
    return [jnp.asarray(np.float32(table)) for table in (along_x, along_y, to_cells, scatter, multiplicity)]


def ghost_index(slots, codes, edge_lists, border_list, count):
    span = len(edge_lists[0])
    result = []
    for facing in range(4):
        for station in range(span):
            source = jnp.zeros_like(codes[facing])
            for code_value in range(8):
                remote = code_value % 4
                mirrored = station if code_value < 4 else span - 1 - station
                source = source + jnp.where(codes[facing] == code_value, border_list.index(edge_lists[remote][mirrored]), 0)
            result.append(source * count + slots[facing])
    return jnp.stack(result).astype(jnp.int32)


def divergence(winds, along_x, along_y):
    return (jnp.einsum("nm,lme->lne", along_x, winds[0], precision=PRECISE)
            + jnp.einsum("nm,lme->lne", along_y, winds[1], precision=PRECISE))


def dynamics_star(winds, surface, column, along_x, along_y):
    surface_star = surface - STEP * column
    grad_x = jnp.dot(along_x, surface_star, precision=PRECISE)
    grad_y = jnp.dot(along_y, surface_star, precision=PRECISE)
    winds_star = winds - STEP * jnp.stack([grad_x, grad_y])[:, None]
    return winds_star, surface_star


def node_border(winds_star, surface_star):
    levels = winds_star.shape[1]
    count = winds_star.shape[3]
    picked = winds_star[:, :, jnp.array(BORDER_NODES), :].reshape(2 * levels, 12, count)
    return jnp.concatenate([picked, surface_star[None, jnp.array(BORDER_NODES), :]], axis=0)


def edge_sums(values, ghosts, scatter, multiplicity):
    total = values + jnp.einsum("ng,rge->rne", scatter, ghosts, precision=PRECISE)
    return total / multiplicity[None, :, None]


def remap_cells(values, ghosts, shift_x, shift_y):
    result = []
    for cell_row in range(3):
        for cell_col in range(3):
            cell_index = 3 * cell_row + cell_col
            middle = values[..., cell_index, :, :]
            west_side = values[..., cell_index - 1, :, :] if cell_col > 0 else ghosts[..., 9 + 2 - cell_row, :, :]
            east_side = values[..., cell_index + 1, :, :] if cell_col < 2 else ghosts[..., 3 + cell_row, :, :]
            south_side = values[..., cell_index - 3, :, :] if cell_row > 0 else ghosts[..., cell_col, :, :]
            north_side = values[..., cell_index + 3, :, :] if cell_row < 2 else ghosts[..., 6 + 2 - cell_col, :, :]
            slope_x = 0.5 * (east_side - west_side)
            curve_x = 0.5 * (east_side + west_side) - middle
            slope_y = 0.5 * (north_side - south_side)
            curve_y = 0.5 * (north_side + south_side) - middle
            moved_x = shift_x[..., cell_index, :, :]
            moved_y = shift_y[..., cell_index, :, :]
            result.append(middle - slope_x * moved_x + curve_x * moved_x * moved_x
                          - slope_y * moved_y + curve_y * moved_y * moved_y)
    return jnp.stack(result, axis=-3)


def reference(winds, surface, thickness, tracers, neighbours, rotations, live_count):
    along_x, along_y, to_cells, scatter, multiplicity = node_tables()
    column = jnp.einsum("l,lne->ne", thickness, divergence(winds, along_x, along_y), precision=PRECISE)
    winds_star, surface_star = dynamics_star(winds, surface, column, along_x, along_y)
    border = node_border(winds_star, surface_star)
    rows_total = border.shape[0]
    node_index = ghost_index(neighbours, rotations, NODE_EDGES, BORDER_NODES, ELEMS)
    ghosts = jnp.take(border.reshape(rows_total, 12 * ELEMS), node_index, axis=1)
    values = jnp.concatenate([winds_star.reshape(2 * NLEV, 16, ELEMS), surface_star[None]], axis=0)
    summed = edge_sums(values, ghosts, scatter, multiplicity)
    winds_new = summed[:2 * NLEV].reshape(2, NLEV, 16, ELEMS)
    surface_new = summed[2 * NLEV]
    shift_x = COURANT * jnp.tanh(jnp.einsum("cn,lne->lce", to_cells, winds_new[0], precision=PRECISE))
    shift_y = COURANT * jnp.tanh(jnp.einsum("cn,lne->lce", to_cells, winds_new[1], precision=PRECISE))
    cell_index = ghost_index(neighbours, rotations, CELL_EDGES, BORDER_CELLS, ELEMS).reshape(-1)

    def one_level(items):
        field, level_x, level_y = items
        border_cells = jnp.concatenate([field[0:4], field[5:9]], axis=0).reshape(8 * ELEMS, NTRAC)
        cell_ghosts = jnp.take(border_cells, cell_index, axis=0).reshape(12, ELEMS, NTRAC)
        return remap_cells(field, cell_ghosts, level_x[:, :, None], level_y[:, :, None])

    moved = lax.map(one_level, (tracers, shift_x, shift_y))
    slot_ids = jnp.arange(ELEMS, dtype=jnp.int32)
    owner_ids = (slot_ids // E_DEV).astype(jnp.int32)
    live = (slot_ids % E_DEV) < jnp.take(live_count, owner_ids)
    winds_out = jnp.where(live, winds_new, 0.0)
    surface_out = jnp.where(live, surface_new, 0.0)
    tracers_out = jnp.where(live[:, None], moved, 0.0)
    return winds_out, surface_out, tracers_out
```

```python
import functools
import jax
import jax.numpy as jnp
import numpy as np
from jax import lax
from jax.experimental import pallas as pl
from jax.experimental.pallas import tpu as pltpu
from jax.sharding import PartitionSpec as P

STEP = 0.1
COURANT = 0.45
HALO = 16
NODE_EDGES = [[0, 1, 2, 3], [3, 7, 11, 15], [15, 14, 13, 12], [12, 8, 4, 0]]
NODE_RING = [0, 1, 2, 3, 7, 11, 15, 14, 13, 12, 8, 4]
CELL_RING = [0, 1, 2, 5, 8, 7, 6, 3]
FIELDS = 8


def tables():
    points = np.array([-1.0, -(0.2**0.5), 0.2**0.5, 1.0])
    products = np.array(
        [np.prod([points[a] - points[k] for k in range(4) if k != a]) for a in range(4)]
    )
    derivative = np.zeros((4, 4))
    for source in range(4):
        for target in range(4):
            if source != target:
                derivative[source, target] = (
                    products[source] / products[target] / (points[source] - points[target])
                )
        derivative[source, source] = sum(
            (1.0 / (points[source] - points[k]) for k in range(4) if k != source)
        )
    identity = np.eye(4)
    along_x = np.kron(identity, derivative)
    along_y = np.kron(derivative, identity)
    centers = np.array([-2.0 / 3.0, 0.0, 2.0 / 3.0])
    lagrange = np.array(
        [
            [
                np.prod([(t - points[k]) / (points[b] - points[k]) for k in range(4) if k != b])
                for b in range(4)
            ]
            for t in centers
        ]
    )
    return along_x.astype(np.float32), along_y.astype(np.float32), lagrange


def multiplicity(node):
    return 1 + sum(node in edge for edge in NODE_EDGES)


def exact_dot(a, b):
    return jnp.dot(a, b, precision=lax.Precision.HIGHEST, preferred_element_type=jnp.float32)


def column_kernel(thickness_in, matrix_in, winds_in, part, thickness, matrix, winds, sems):
    copies = [
        pltpu.make_async_copy(source, target, sems.at[number])
        for number, (source, target) in enumerate(
            ((winds_in, winds), (matrix_in, matrix), (thickness_in, thickness))
        )
    ]
    for copy in copies:
        copy.start()
    for copy in copies:
        copy.wait()
    levels = winds.shape[1]
    sums = []
    for component in range(2):
        total = thickness[0] * winds[component, 0]
        for level in range(1, levels):
            total = total + thickness[level] * winds[component, level]
        sums.append(total)
    part[...] = exact_dot(matrix[...], jnp.concatenate(sums, axis=0))


def strips(live):
    even = lax.rem(lax.axis_index("elem"), 2) == 0
    start = live[0] - HALO
    tile = start // 128
    lane = start % 128
    return (
        (jnp.where(even, tile, 0), jnp.where(even, lane, 0)),
        (jnp.where(even, 0, tile), jnp.where(even, 0, lane)),
    )


def strip_kernel(live, tracers, order, held, inside, outside, sems):
    del order
    levels, _, tracer_total, _ = tracers.shape
    loads = [
        pltpu.make_async_copy(tracers.at[level], held.at[level], sems.at[level])
        for level in range(levels)
    ]
    for load in loads:
        load.start()
    lane_block = lax.broadcasted_iota(jnp.int32, (8, 128), 1) // HALO
    ends = strips(live)
    for level in range(levels):
        loads[level].wait()
        for target, (tile, lane) in zip((inside, outside), ends):
            lanes = pl.ds(pl.multiple_of(128 * tile, 128), 128)
            shifts = [lax.rem(HALO * place + 128 - lane, 128) for place in range(8)]

            def pack(group, carry, target=target, lanes=lanes, shifts=shifts, level=level):
                base = pl.multiple_of(8 * group, 8)
                packed = None
                for place in range(8):
                    values = held[level, CELL_RING[place], pl.ds(base, 8), lanes]
                    moved = pltpu.roll(values, shifts[place], 1)
                    packed = (
                        moved if packed is None else jnp.where(lane_block == place, moved, packed)
                    )
                target[pl.ds(level * tracer_total + base, 8), :] = packed
                return carry

            lax.fori_loop(0, tracer_total // 8, pack, 0, unroll=4)


def star_kernel(live, matrix, *refs):
    *parts, surface, winds, inside_in, outside_in, star, inside, outside = refs
    del inside_in, outside_in
    levels = winds.shape[1]
    column = parts[0][...]
    for part in parts[1:]:
        column = column + part[...]
    surface_star = surface[...] - STEP * column
    gradient = exact_dot(matrix[...], surface_star)
    for tile in range(2):
        lanes = slice(128 * tile, 128 * tile + 128)
        for component in range(2):
            slope = gradient[16 * component : 16 * component + 16, lanes]
            for level in range(levels):
                star[tile, pl.ds(levels * component + level, 16, stride=FIELDS), :] = (
                    winds[component, level, :, lanes] - STEP * slope
                )
        for field in range(2 * levels, FIELDS):
            star[tile, pl.ds(field, 16, stride=FIELDS), :] = surface_star[:, lanes]
    lane_block = lax.broadcasted_iota(jnp.int32, (FIELDS, 128), 1) // HALO
    base = inside.shape[0] - 2 * FIELDS
    for target, (tile, at) in zip((inside, outside), strips(live)):
        for block in range(2):
            packed = None
            for place in range(min(8, 12 - 8 * block)):
                node = NODE_RING[8 * block + place]
                values = star[tile, pl.ds(FIELDS * node, FIELDS), :]
                moved = pltpu.roll(values, lax.rem(HALO * place + 128 - at, 128), 1)
                packed = moved if packed is None else jnp.where(lane_block == place, moved, packed)
            target[pl.ds(base + FIELDS * block, FIELDS), :] = packed


def add_edges(nodes, codes, ring):
    for edge in range(4):
        code = codes[edge]
        found = ring(edge)
        for place in range(4):
            value = found((3 - place) % 12)
            for other in range(1, 4):
                value = jnp.where(code == other, found((3 * other + 3 - place) % 12), value)
            node = NODE_EDGES[edge][place]
            nodes[node] = nodes[node] + value


def rows_of(ref, edge, tile):
    return jnp.broadcast_to(ref[pl.ds(edge, 1), pl.ds(128 * tile, 128)], (FIELDS, 128))


def lane_gather(values, index):
    return jnp.take_along_axis(values, index, axis=1, mode="promise_in_bounds")


def weights(nodes, live, tile, factors):
    lagrange = tables()[2]
    rows = [
        [
            sum(float(lagrange[x, n]) * nodes[4 * y + n] for n in range(4))
            for x in range(3)
        ]
        for y in range(4)
    ]
    lanes = pl.ds(128 * tile, 128)
    lane = lax.broadcasted_iota(jnp.int32, (FIELDS, 128), 1) + 128 * tile
    row = lax.broadcasted_iota(jnp.int32, (FIELDS, 128), 0)
    alive = lane < live
    for y in range(3):
        for x in range(3):
            value = sum(float(lagrange[y, n]) * rows[n][x] for n in range(4))
            shift = COURANT * jnp.tanh(value)
            square = shift * shift
            low = 0.5 * (square + shift)
            high = 0.5 * (square - shift)
            middle = 1.0 - square - pltpu.roll(square, 6, 0)
            sides = jnp.where(row < 4, low, pltpu.roll(high, 4, 0))
            at = 16 * (3 * y + x)
            factors[pl.ds(at, 8), lanes] = jnp.where(alive, sides, 0.0)
            factors[pl.ds(at + 8, 8), lanes] = jnp.where(alive, middle, 0.0)


def picks(line, wanted):
    return jnp.where(line == wanted, 1.0, 0.0).astype(jnp.bfloat16)


def split(values):
    high = values.astype(jnp.bfloat16)
    low = (values - high.astype(jnp.float32)).astype(jnp.bfloat16)
    return jnp.concatenate([high, low], axis=1)


def inner_kernel(neighbours, rotations, star, held, order, sums, ghosts, remote):
    del order
    levels, _, tracer_total, count = held.shape
    me = lax.axis_index("elem")
    for tile in range(2):
        nodes = [star[tile, pl.ds(FIELDS * n, FIELDS), :] for n in range(16)]
        codes = [rows_of(rotations, edge, tile) & 3 for edge in range(4)]

        def ring(edge, tile=tile):
            slots = rows_of(neighbours, edge, tile)
            own = slots // count == me
            local = slots % count
            within = local % 128
            upper = local >= 128
            kept = {}

            def found(place):
                if place not in kept:
                    at = pl.ds(FIELDS * NODE_RING[place], FIELDS)
                    both = jnp.where(
                        upper, lane_gather(star[1, at, :], within), lane_gather(star[0, at, :], within)
                    )
                    kept[place] = jnp.where(own, both, 0.0)
                return kept[place]

            return found

        add_edges(nodes, codes, ring)
        for n in range(16):
            sums[tile, pl.ds(FIELDS * n, FIELDS), :] = nodes[n]

    devices = lax.axis_size("elem")
    line = lax.broadcasted_iota(jnp.int32, (count, count), 0)
    slots = neighbours[...]
    own = slots // count == me
    after = slots // count == lax.rem(me + 1, devices)
    codes = rotations[...] & 3
    near = jnp.where(own, slots % count, -1)
    pickers = []
    for edge in range(4):
        picker = picks(line, near[edge : edge + 1])
        pickers.append(jnp.concatenate([picker, picker], axis=0))
    for place in range(3):
        source = HALO * ((2 * codes + 2 - place) & 7) + slots % HALO + jnp.where(after, 128, 0)
        source = jnp.where(own, -1, source)
        for edge in range(4):
            remote[3 * edge + place] = picks(line, source[edge : edge + 1])
    chosen = [
        [jnp.broadcast_to(codes[edge : edge + 1] == other, (8, count)) for other in range(4)]
        for edge in range(4)
    ]
    for level in range(levels):
        for start in range(0, tracer_total, BLOCK):
            rows = pl.ds(start, BLOCK)
            border = jnp.concatenate([split(held[level, cell, rows, :]) for cell in CELL_RING], axis=0)
            for edge in range(4):
                ring = jnp.dot(border, pickers[edge], preferred_element_type=jnp.float32)
                for at in range(0, BLOCK, 8):
                    for place in range(3):
                        value = None
                        for other in range(4):
                            base = BLOCK * ((2 * other + 2 - place) % 8) + at
                            found = ring[base : base + 8]
                            value = found if value is None else jnp.where(chosen[edge][other], found, value)
                        ghosts[level, 3 * edge + place, pl.ds(start + at, 8), :] = value


def outer_kernel(
    live,
    neighbours,
    rotations,
    sums,
    held,
    near,
    remote,
    inside,
    outside,
    winds_out,
    surface_out,
    moved,
    means,
    factors,
    ghosts,
    done,
    sems,
):
    levels, _, tracer_total, count = held.shape
    me = lax.axis_index("elem")
    devices = lax.axis_size("elem")
    even = lax.rem(me, 2) == 0
    base = levels * tracer_total

    def both_sides(rows):
        left, right = inside[rows, :], outside[rows, :]
        return jnp.where(even, right, left), jnp.where(even, left, right)

    strip = split(jnp.concatenate(both_sides(pl.ds(0, base)), axis=1))
    for number in range(12):
        picker = remote[number]
        found = jnp.dot(
            strip, jnp.concatenate([picker, picker], axis=0), preferred_element_type=jnp.float32
        )
        for level in range(levels):
            ghosts[level, number] = near[level, number] + found[level * tracer_total : (level + 1) * tracer_total]

    node_halo = [both_sides(pl.ds(base + FIELDS * block, FIELDS)) for block in range(2)]
    for tile in range(2):
        nodes = [sums[tile, pl.ds(FIELDS * n, FIELDS), :] for n in range(16)]
        for edge in range(4):
            slots = rows_of(neighbours, edge, tile)
            code = rows_of(rotations, edge, tile) & 3
            owner = slots // count
            other = owner != me
            after = owner == lax.rem(me + 1, devices)
            for place in range(4):
                spot = 3 * code + 3 - place
                spot = jnp.where(spot >= 12, spot - 12, spot)
                index = HALO * (spot & 7) + (slots & (HALO - 1))
                high = spot >= 8
                value = jnp.where(
                    high, lane_gather(node_halo[1][1], index), lane_gather(node_halo[0][1], index)
                )
                if tile == 0:
                    behind = jnp.where(
                        high, lane_gather(node_halo[1][0], index), lane_gather(node_halo[0][0], index)
                    )
                    value = jnp.where(after, value, behind)
                node = NODE_EDGES[edge][place]
                nodes[node] = nodes[node] + jnp.where(other, value, 0.0)
        nodes = [nodes[n] * (1.0 / multiplicity(n)) for n in range(16)]
        weights(nodes, live[0], tile, factors)
        lane = lax.broadcasted_iota(jnp.int32, (FIELDS, 128), 1) + 128 * tile
        for n in range(16):
            means[tile, pl.ds(FIELDS * n, FIELDS), :] = jnp.where(lane < live[0], nodes[n], 0.0)
        lanes = pl.ds(128 * tile, 128)
        for component in range(2):
            for level in range(levels):
                winds_out[component, level, :, lanes] = means[
                    tile, pl.ds(levels * component + level, 16, stride=FIELDS), :
                ]
        surface_out[:, lanes] = means[tile, pl.ds(2 * levels, 16, stride=FIELDS), :]

    chunk = CHUNK
    for level in range(levels):

        def groups(group, carry, level=level):
            rows = [pl.ds(pl.multiple_of(chunk * group + 8 * i, 8), 8) for i in range(chunk // 8)]
            for tile in range(2):
                lanes = pl.ds(128 * tile, 128)

                def ghost(edge, place):
                    return [ghosts[level, 3 * edge + place, r, lanes] for r in rows]

                cells = [[held[level, cell, r, lanes] for r in rows] for cell in range(9)]
                for row in range(3):
                    for col in range(3):
                        cell = 3 * row + col
                        west = cells[cell - 1] if col > 0 else ghost(3, 2 - row)
                        east = cells[cell + 1] if col < 2 else ghost(1, row)
                        south = cells[cell - 3] if row > 0 else ghost(0, col)
                        north = cells[cell + 3] if row < 2 else ghost(2, 2 - col)
                        factor = [
                            jnp.broadcast_to(factors[pl.ds(16 * cell + at + level, 1), lanes], (8, 128))
                            for at in (0, 2, 4, 6, 8)
                        ]
                        for i, r in enumerate(rows):
                            done[level, cell, r, lanes] = (
                                cells[cell][i] * factor[4]
                                + (west[i] * factor[0] + east[i] * factor[2])
                                + (south[i] * factor[1] + north[i] * factor[3])
                            )
            where = (level, slice(None), pl.ds(pl.multiple_of(chunk * group, 8), chunk))
            pltpu.make_async_copy(done.at[where], moved.at[where], sems.at[level, group]).start()
            return carry

        lax.fori_loop(0, tracer_total // chunk, groups, 0)
    for level in range(levels):
        for group in range(tracer_total // chunk):
            where = (level, slice(None), pl.ds(chunk * group, chunk))
            pltpu.make_async_copy(done.at[where], moved.at[where], sems.at[level, group]).wait()


VMEM = pl.BlockSpec(memory_space=pltpu.VMEM)
SMEM = pl.BlockSpec(memory_space=pltpu.SMEM)
HBM = pl.BlockSpec(memory_space=pltpu.HBM)
ANY = pl.BlockSpec(memory_space=pl.ANY)
LIMIT = pltpu.CompilerParams(vmem_limit_bytes=20 * 1024 * 1024)
CHUNK = 32
BLOCK = 112


def in_hbm(array):
    return pltpu.with_memory_space_constraint(array, pltpu.HBM)


def body(winds, surface, thickness, tracers, neighbours, rotations, live_count):
    levels, _, count, tracer_total = tracers.shape
    along_x, along_y, _ = tables()
    across = jnp.asarray(np.concatenate([along_x, along_y], axis=1))
    down = jnp.asarray(np.concatenate([along_x, along_y], axis=0))
    f32 = functools.partial(jax.ShapeDtypeStruct, dtype=jnp.float32)
    turned = jnp.transpose(tracers, (0, 1, 3, 2))
    pack_shape = (levels * tracer_total + 2 * FIELDS, 128)

    part = pl.pallas_call(
        column_kernel,
        name="column",
        in_specs=[HBM, HBM, HBM],
        out_specs=VMEM,
        out_shape=f32((16, count)),
        scratch_shapes=[
            pltpu.SMEM(thickness.shape, jnp.float32),
            pltpu.VMEM(across.shape, jnp.float32),
            pltpu.VMEM(winds.shape, jnp.float32),
            pltpu.SemaphoreType.DMA((3,)),
        ],
        compiler_params=LIMIT,
    )(in_hbm(thickness), in_hbm(across), in_hbm(winds))

    ranks = lax.axis_size("lev")
    parts = [part]
    for step in range(1, ranks):
        parts.append(lax.ppermute(part, "lev", [(i, i ^ step) for i in range(ranks)]))

    held, inside, outside = pl.pallas_call(
        strip_kernel,
        name="strips",
        in_specs=[SMEM, HBM, ANY],
        out_specs=[VMEM] * 3,
        out_shape=[
            pltpu.VMEM(turned.shape, jnp.float32),
            pltpu.VMEM(pack_shape, jnp.float32),
            pltpu.VMEM(pack_shape, jnp.float32),
        ],
        scratch_shapes=[pltpu.SemaphoreType.DMA((levels,))],
        compiler_params=LIMIT,
    )(live_count, in_hbm(turned), part)

    star, inside, outside = pl.pallas_call(
        star_kernel,
        name="star",
        in_specs=[SMEM, VMEM] + [VMEM] * (ranks + 4),
        out_specs=[VMEM] * 3,
        out_shape=[
            pltpu.VMEM((2, 16 * FIELDS, 128), jnp.float32),
            pltpu.VMEM(pack_shape, jnp.float32),
            pltpu.VMEM(pack_shape, jnp.float32),
        ],
        input_output_aliases={ranks + 4: 1, ranks + 5: 2},
        compiler_params=LIMIT,
    )(live_count, down, *parts, surface, winds, inside, outside)

    devices = lax.axis_size("elem")
    outside_in = lax.ppermute(
        outside, "elem", [(i, (((i + 1) % devices ^ 1) - 1) % devices) for i in range(devices)]
    )
    inside_in = lax.ppermute(inside, "elem", [(i, i ^ 1) for i in range(devices)])

    sums, ghosts, remote = pl.pallas_call(
        inner_kernel,
        name="inner",
        in_specs=[VMEM, VMEM, VMEM, VMEM, ANY],
        out_specs=[VMEM, VMEM, VMEM],
        out_shape=[
            pltpu.VMEM((2, 16 * FIELDS, 128), jnp.float32),
            pltpu.VMEM((levels, 12, tracer_total, count), jnp.float32),
            pltpu.VMEM((12, count, count), jnp.bfloat16),
        ],
        compiler_params=LIMIT,
    )(neighbours, rotations, star, held, star)

    winds_out, surface_out, moved = pl.pallas_call(
        outer_kernel,
        name="outer",
        in_specs=[SMEM] + [VMEM] * 8,
        out_specs=[VMEM, VMEM, HBM],
        out_shape=[f32(winds.shape), f32(surface.shape), f32(turned.shape)],
        scratch_shapes=[
            pltpu.VMEM((2, 16 * FIELDS, 128), jnp.float32),
            pltpu.VMEM((9 * 16, count), jnp.float32),
            pltpu.VMEM((levels, 12, tracer_total, count), jnp.float32),
            pltpu.VMEM(turned.shape, jnp.float32),
            pltpu.SemaphoreType.DMA((levels, tracer_total // CHUNK)),
        ],
        compiler_params=LIMIT,
    )(live_count, neighbours, rotations, sums, held, ghosts, remote, inside_in, outside_in)
    return winds_out, surface_out, jnp.transpose(moved, (0, 1, 3, 2))


def solution(mesh):
    in_specs = (
        P(None, "lev", None, "elem"),
        P(None, "elem"),
        P("lev"),
        P("lev", None, "elem", None),
        P(None, "elem"),
        P(None, "elem"),
        P("elem"),
    )
    out_specs = (P(None, "lev", None, "elem"), P(None, "elem"), P("lev", None, "elem", None))
    return jax.shard_map(body, mesh=mesh, in_specs=in_specs, out_specs=out_specs, check_vma=False)
```

```python
import functools
import jax
import jax.numpy as jnp
import numpy as np
from jax import lax
from jax.experimental import pallas as pl
from jax.experimental.pallas import tpu as pltpu
from jax.sharding import PartitionSpec as P

STEP = 0.1
COURANT = 0.45
HALO = 16
NODE_EDGES = [[0, 1, 2, 3], [3, 7, 11, 15], [15, 14, 13, 12], [12, 8, 4, 0]]
NODE_RING = [0, 1, 2, 3, 7, 11, 15, 14, 13, 12, 8, 4]
CELL_RING = [0, 1, 2, 5, 8, 7, 6, 3]
FIELDS = 8


def tables():
    points = np.array([-1.0, -(0.2**0.5), 0.2**0.5, 1.0])
    products = np.array(
        [np.prod([points[a] - points[k] for k in range(4) if k != a]) for a in range(4)]
    )
    derivative = np.zeros((4, 4))
    for source in range(4):
        for target in range(4):
            if source != target:
                derivative[source, target] = (
                    products[source] / products[target] / (points[source] - points[target])
                )
        derivative[source, source] = sum(
            (1.0 / (points[source] - points[k]) for k in range(4) if k != source)
        )
    identity = np.eye(4)
    along_x = np.kron(identity, derivative)
    along_y = np.kron(derivative, identity)
    centers = np.array([-2.0 / 3.0, 0.0, 2.0 / 3.0])
    lagrange = np.array(
        [
            [
                np.prod([(t - points[k]) / (points[b] - points[k]) for k in range(4) if k != b])
                for b in range(4)
            ]
            for t in centers
        ]
    )
    return along_x.astype(np.float32), along_y.astype(np.float32), lagrange


def multiplicity(node):
    return 1 + sum(node in edge for edge in NODE_EDGES)


def exact_dot(a, b):
    return jnp.dot(a, b, precision=lax.Precision.HIGHEST, preferred_element_type=jnp.float32)


def column_kernel(thickness_in, matrix_in, winds_in, part, thickness, matrix, winds, sems):
    copies = [
        pltpu.make_async_copy(source, target, sems.at[number])
        for number, (source, target) in enumerate(
            ((winds_in, winds), (matrix_in, matrix), (thickness_in, thickness))
        )
    ]
    for copy in copies:
        copy.start()
    for copy in copies:
        copy.wait()
    levels = winds.shape[1]
    sums = []
    for component in range(2):
        total = thickness[0] * winds[component, 0]
        for level in range(1, levels):
            total = total + thickness[level] * winds[component, level]
        sums.append(total)
    part[...] = exact_dot(matrix[...], jnp.concatenate(sums, axis=0))


def first_of(ref):
    return ref[...][0]


def strips(live):
    even = lax.rem(lax.axis_index("elem"), 2) == 0
    start = first_of(live) - HALO
    tile = start // 128
    lane = start % 128
    return (
        (jnp.where(even, tile, 0), jnp.where(even, lane, 0)),
        (jnp.where(even, 0, tile), jnp.where(even, 0, lane)),
    )


def picks(line, wanted):
    return jnp.where(line == wanted, 1.0, 0.0).astype(jnp.bfloat16)


def split(values):
    high = values.astype(jnp.bfloat16)
    low = (values - high.astype(jnp.float32)).astype(jnp.bfloat16)
    return jnp.concatenate([high, low], axis=1)


def strip_kernel(live, tracers, order, held, border, inside, outside, sems):
    del order
    levels, _, tracer_total, count = tracers.shape
    loads = [
        pltpu.make_async_copy(tracers.at[level], held.at[level], sems.at[level])
        for level in range(levels)
    ]
    for load in loads:
        load.start()
    line = lax.broadcasted_iota(jnp.int32, (count, 256), 0)
    lane = lax.broadcasted_iota(jnp.int32, (count, 256), 1)
    starts = [128 * tile + at for tile, at in strips(live)]
    picker = picks(line, jnp.where(lane < 128, starts[0], starts[1]) + lane % HALO)
    picker = jnp.concatenate([picker, picker], axis=0)
    part = (lax.broadcasted_iota(jnp.int32, (BLOCK, 256), 1) % 128) // HALO
    for level in range(levels):
        loads[level].wait()
        for block in range(tracer_total // BLOCK):
            rows = pl.ds(BLOCK * block, BLOCK)
            for place, cell in enumerate(CELL_RING):
                border[level, block, pl.ds(BLOCK * place, BLOCK), :] = split(held[level, cell, rows, :])
            found = jnp.dot(border[level, block], picker, preferred_element_type=jnp.float32)
            packed = found[:BLOCK]
            for place in range(1, 8):
                packed = jnp.where(part == place, found[BLOCK * place : BLOCK * (place + 1)], packed)
            rows = pl.ds(level * tracer_total + BLOCK * block, BLOCK)
            inside[rows, :] = packed[:, :128]
            outside[rows, :] = packed[:, 128:]


def star_kernel(live, matrix, *refs):
    *parts, surface, winds, neighbours, rotations, border, inside_in, outside_in = refs[:-4]
    star, inside, outside, ghosts = refs[-4:]
    del inside_in, outside_in
    levels = winds.shape[1]
    column = parts[0][...]
    for part in parts[1:]:
        column = column + part[...]
    surface_star = surface[...] - STEP * column
    gradient = exact_dot(matrix[...], surface_star)
    for tile in range(2):
        lanes = slice(128 * tile, 128 * tile + 128)
        for component in range(2):
            slope = gradient[16 * component : 16 * component + 16, lanes]
            for level in range(levels):
                star[tile, pl.ds(levels * component + level, 16, stride=FIELDS), :] = (
                    winds[component, level, :, lanes] - STEP * slope
                )
        for field in range(2 * levels, FIELDS):
            star[tile, pl.ds(field, 16, stride=FIELDS), :] = surface_star[:, lanes]
    lane_block = lax.broadcasted_iota(jnp.int32, (FIELDS, 128), 1) // HALO
    base = inside.shape[0] - 2 * FIELDS
    for target, (tile, at) in zip((inside, outside), strips(live)):
        for block in range(2):
            packed = None
            for place in range(min(8, 12 - 8 * block)):
                node = NODE_RING[8 * block + place]
                values = star[tile, pl.ds(FIELDS * node, FIELDS), :]
                moved = pltpu.roll(values, lax.rem(HALO * place + 128 - at, 128), 1)
                packed = moved if packed is None else jnp.where(lane_block == place, moved, packed)
            target[pl.ds(base + FIELDS * block, FIELDS), :] = packed

    @pl.when(lax.axis_index("elem") == 0)
    def _():
        near_ghosts(neighbours, rotations, border, ghosts, range(1))


def add_edges(nodes, codes, ring):
    for edge in range(4):
        code = codes[edge]
        found = ring(edge)
        for place in range(4):
            value = found((3 - place) % 12)
            for other in range(1, 4):
                value = jnp.where(code == other, found((3 * other + 3 - place) % 12), value)
            node = NODE_EDGES[edge][place]
            nodes[node] = nodes[node] + value


def rows_of(ref, edge, tile):
    return jnp.broadcast_to(ref[pl.ds(edge, 1), pl.ds(128 * tile, 128)], (FIELDS, 128))


def lane_gather(values, index):
    return jnp.take_along_axis(values, index, axis=1, mode="promise_in_bounds")


def weights(nodes, live, tile, factors):
    lagrange = tables()[2]
    rows = [
        [
            sum(float(lagrange[x, n]) * nodes[4 * y + n] for n in range(4))
            for x in range(3)
        ]
        for y in range(4)
    ]
    lanes = pl.ds(128 * tile, 128)
    lane = lax.broadcasted_iota(jnp.int32, (FIELDS, 128), 1) + 128 * tile
    row = lax.broadcasted_iota(jnp.int32, (FIELDS, 128), 0)
    alive = lane < live
    for y in range(3):
        for x in range(3):
            value = sum(float(lagrange[y, n]) * rows[n][x] for n in range(4))
            shift = COURANT * jnp.tanh(value)
            square = shift * shift
            low = 0.5 * (square + shift)
            high = 0.5 * (square - shift)
            middle = 1.0 - square - pltpu.roll(square, 6, 0)
            sides = jnp.where(row < 4, low, pltpu.roll(high, 4, 0))
            at = 16 * (3 * y + x)
            factors[pl.ds(at, 8), lanes] = jnp.where(alive, sides, 0.0)
            factors[pl.ds(at + 8, 8), lanes] = jnp.where(alive, middle, 0.0)


def near_ghosts(neighbours, rotations, border, ghosts, which):
    count = ghosts.shape[3]
    me = lax.axis_index("elem")
    line = lax.broadcasted_iota(jnp.int32, (count, count), 0)
    slots = neighbours[...]
    codes = rotations[...] & 3
    near = jnp.where(slots // count == me, slots % count, -1)
    pickers = []
    for edge in range(4):
        picker = picks(line, near[edge : edge + 1])
        pickers.append(jnp.concatenate([picker, picker], axis=0))
    chosen = [
        [jnp.broadcast_to(codes[edge : edge + 1] == other, (8, count)) for other in range(4)]
        for edge in range(4)
    ]
    for level in which:
        for block in range(border.shape[1]):
            for edge in range(4):
                ring = jnp.dot(border[level, block], pickers[edge], preferred_element_type=jnp.float32)
                for at in range(0, BLOCK, 8):
                    for place in range(3):
                        value = None
                        for other in range(4):
                            base = BLOCK * ((2 * other + 2 - place) % 8) + at
                            found = ring[base : base + 8]
                            value = found if value is None else jnp.where(chosen[edge][other], found, value)
                        ghosts[level, 3 * edge + place, pl.ds(BLOCK * block + at, 8), :] = value


def inner_kernel(neighbours, rotations, star, border, begun, order, sums, ghosts, remote):
    del begun, order
    levels, _, tracer_total, count = ghosts.shape
    me = lax.axis_index("elem")
    for tile in range(2):
        nodes = [star[tile, pl.ds(FIELDS * n, FIELDS), :] for n in range(16)]
        codes = [rows_of(rotations, edge, tile) & 3 for edge in range(4)]

        def ring(edge, tile=tile):
            slots = rows_of(neighbours, edge, tile)
            own = slots // count == me
            local = slots % count
            within = local % 128
            upper = local >= 128
            kept = {}

            def found(place):
                if place not in kept:
                    at = pl.ds(FIELDS * NODE_RING[place], FIELDS)
                    both = jnp.where(
                        upper, lane_gather(star[1, at, :], within), lane_gather(star[0, at, :], within)
                    )
                    kept[place] = jnp.where(own, both, 0.0)
                return kept[place]

            return found

        add_edges(nodes, codes, ring)
        for n in range(16):
            sums[tile, pl.ds(FIELDS * n, FIELDS), :] = nodes[n]

    devices = lax.axis_size("elem")
    line = lax.broadcasted_iota(jnp.int32, (count, count), 0)
    slots = neighbours[...]
    own = slots // count == me
    after = slots // count == lax.rem(me + 1, devices)
    codes = rotations[...] & 3
    for place in range(3):
        source = HALO * ((2 * codes + 2 - place) & 7) + slots % HALO + jnp.where(after, 128, 0)
        source = jnp.where(own, -1, source)
        for edge in range(4):
            remote[3 * edge + place] = picks(line, source[edge : edge + 1])

    @pl.when(me != 0)
    def _():
        near_ghosts(neighbours, rotations, border, ghosts, range(1))

    near_ghosts(neighbours, rotations, border, ghosts, range(1, levels))


def outer_kernel(
    live,
    neighbours,
    rotations,
    sums,
    held,
    near,
    remote,
    inside,
    outside,
    winds_out,
    surface_out,
    moved,
    means,
    factors,
    winds_new,
    surface_new,
    done,
    sems,
):
    levels, _, tracer_total, count = held.shape
    me = lax.axis_index("elem")
    devices = lax.axis_size("elem")
    even = lax.rem(me, 2) == 0
    alive = first_of(live)
    base = levels * tracer_total

    def both_sides(rows):
        left, right = inside[rows, :], outside[rows, :]
        return jnp.where(even, right, left), jnp.where(even, left, right)

    node_halo = [both_sides(pl.ds(base + FIELDS * block, FIELDS)) for block in range(2)]
    for tile in range(2):
        nodes = [sums[tile, pl.ds(FIELDS * n, FIELDS), :] for n in range(16)]
        for edge in range(4):
            slots = rows_of(neighbours, edge, tile)
            code = rows_of(rotations, edge, tile) & 3
            owner = slots // count
            other = owner != me
            after = owner == lax.rem(me + 1, devices)
            for place in range(4):
                spot = 3 * code + 3 - place
                spot = jnp.where(spot >= 12, spot - 12, spot)
                index = HALO * (spot & 7) + (slots & (HALO - 1))
                high = spot >= 8
                value = jnp.where(
                    high, lane_gather(node_halo[1][1], index), lane_gather(node_halo[0][1], index)
                )
                if tile == 0:
                    behind = jnp.where(
                        high, lane_gather(node_halo[1][0], index), lane_gather(node_halo[0][0], index)
                    )
                    value = jnp.where(after, value, behind)
                node = NODE_EDGES[edge][place]
                nodes[node] = nodes[node] + jnp.where(other, value, 0.0)
        nodes = [nodes[n] * (1.0 / multiplicity(n)) for n in range(16)]
        weights(nodes, alive, tile, factors)
        lane = lax.broadcasted_iota(jnp.int32, (FIELDS, 128), 1) + 128 * tile
        for n in range(16):
            means[tile, pl.ds(FIELDS * n, FIELDS), :] = jnp.where(lane < alive, nodes[n], 0.0)
        lanes = pl.ds(128 * tile, 128)
        for component in range(2):
            for level in range(levels):
                winds_new[component, level, :, lanes] = means[
                    tile, pl.ds(levels * component + level, 16, stride=FIELDS), :
                ]
        surface_new[:, lanes] = means[tile, pl.ds(2 * levels, 16, stride=FIELDS), :]

    copies = [
        pltpu.make_async_copy(winds_new, winds_out, sems.at[levels, 0]),
        pltpu.make_async_copy(surface_new, surface_out, sems.at[levels, 1]),
    ]
    for copy in copies:
        copy.start()

    strip = split(jnp.concatenate(both_sides(pl.ds(0, base)), axis=1))

    def ghost(edge, place):
        number = 3 * edge + place
        picker = remote[number]
        found = jnp.dot(
            strip, jnp.concatenate([picker, picker], axis=0), preferred_element_type=jnp.float32
        )
        return [
            near[level, number] + found[level * tracer_total : (level + 1) * tracer_total]
            for level in range(levels)
        ]

    def own(cell):
        return [held[level, cell] for level in range(levels)]

    for cell in CELL_ORDER:
        row, col = cell // 3, cell % 3
        west = own(cell - 1) if col > 0 else ghost(3, 2 - row)
        east = own(cell + 1) if col < 2 else ghost(1, row)
        south = own(cell - 3) if row > 0 else ghost(0, col)
        north = own(cell + 3) if row < 2 else ghost(2, 2 - col)
        for level in range(levels):
            factor = [factors[pl.ds(16 * cell + at + level, 1), :] for at in (0, 2, 4, 6, 8)]
            done[level, cell] = (
                held[level, cell] * factor[4]
                + (west[level] * factor[0] + east[level] * factor[2])
                + (south[level] * factor[1] + north[level] * factor[3])
            )
            copy = pltpu.make_async_copy(done.at[level, cell], moved.at[level, cell], sems.at[level, cell])
            copy.start()
            copies.append(copy)
    for copy in copies:
        copy.wait()


VMEM = pl.BlockSpec(memory_space=pltpu.VMEM)
SMEM = pl.BlockSpec(memory_space=pltpu.SMEM)
HBM = pl.BlockSpec(memory_space=pltpu.HBM)
ANY = pl.BlockSpec(memory_space=pl.ANY)
LIMIT = pltpu.CompilerParams(vmem_limit_bytes=20 * 1024 * 1024)
CELL_ORDER = [4, 1, 3, 5, 7, 0, 2, 6, 8]
BLOCK = 112


def in_hbm(array):
    return pltpu.with_memory_space_constraint(array, pltpu.HBM)


def body(winds, surface, thickness, tracers, neighbours, rotations, live_count):
    levels, _, count, tracer_total = tracers.shape
    along_x, along_y, _ = tables()
    across = jnp.asarray(np.concatenate([along_x, along_y], axis=1))
    down = jnp.asarray(np.concatenate([along_x, along_y], axis=0))
    f32 = functools.partial(jax.ShapeDtypeStruct, dtype=jnp.float32)
    turned = jnp.transpose(tracers, (0, 1, 3, 2))
    pack_shape = (levels * tracer_total + 2 * FIELDS, 128)

    part = pl.pallas_call(
        column_kernel,
        name="column",
        in_specs=[HBM] * 3,
        out_specs=VMEM,
        out_shape=f32((16, count)),
        scratch_shapes=[
            pltpu.SMEM(thickness.shape, jnp.float32),
            pltpu.VMEM(across.shape, jnp.float32),
            pltpu.VMEM(winds.shape, jnp.float32),
            pltpu.SemaphoreType.DMA((3,)),
        ],
        compiler_params=LIMIT,
    )(in_hbm(thickness), in_hbm(across), in_hbm(winds))

    ranks = lax.axis_size("lev")
    parts = [part]
    for step in range(1, ranks):
        parts.append(lax.ppermute(part, "lev", [(i, i ^ step) for i in range(ranks)]))

    held, border, inside, outside = pl.pallas_call(
        strip_kernel,
        name="strips",
        in_specs=[VMEM, HBM, ANY],
        out_specs=[VMEM] * 4,
        out_shape=[
            pltpu.VMEM(turned.shape, jnp.float32),
            pltpu.VMEM((levels, tracer_total // BLOCK, 8 * BLOCK, 2 * count), jnp.bfloat16),
            pltpu.VMEM(pack_shape, jnp.float32),
            pltpu.VMEM(pack_shape, jnp.float32),
        ],
        scratch_shapes=[pltpu.SemaphoreType.DMA((levels,))],
        compiler_params=LIMIT,
    )(live_count, in_hbm(turned), part)

    ghosts_shape = pltpu.VMEM((levels, 12, tracer_total, count), jnp.float32)
    star, inside, outside, ghosts = pl.pallas_call(
        star_kernel,
        name="star",
        in_specs=[VMEM, VMEM] + [VMEM] * (ranks + 7),
        out_specs=[VMEM] * 4,
        out_shape=[
            pltpu.VMEM((2, 16 * FIELDS, 128), jnp.float32),
            pltpu.VMEM(pack_shape, jnp.float32),
            pltpu.VMEM(pack_shape, jnp.float32),
            ghosts_shape,
        ],
        input_output_aliases={ranks + 7: 1, ranks + 8: 2},
        compiler_params=LIMIT,
    )(live_count, down, *parts, surface, winds, neighbours, rotations, border, inside, outside)

    devices = lax.axis_size("elem")
    outside_in = lax.ppermute(
        outside, "elem", [(i, (((i + 1) % devices ^ 1) - 1) % devices) for i in range(devices)]
    )
    inside_in = lax.ppermute(inside, "elem", [(i, i ^ 1) for i in range(devices)])

    sums, ghosts, remote = pl.pallas_call(
        inner_kernel,
        name="inner",
        in_specs=[VMEM] * 5 + [ANY],
        input_output_aliases={4: 1},
        out_specs=[VMEM, VMEM, VMEM],
        out_shape=[
            pltpu.VMEM((2, 16 * FIELDS, 128), jnp.float32),
            ghosts_shape,
            pltpu.VMEM((12, count, count), jnp.bfloat16),
        ],
        compiler_params=LIMIT,
    )(neighbours, rotations, star, border, ghosts, star)

    winds_out, surface_out, moved = pl.pallas_call(
        outer_kernel,
        name="outer",
        in_specs=[VMEM] + [VMEM] * 8,
        out_specs=[HBM] * 3,
        out_shape=[f32(winds.shape), f32(surface.shape), f32(turned.shape)],
        scratch_shapes=[
            pltpu.VMEM((2, 16 * FIELDS, 128), jnp.float32),
            pltpu.VMEM((9 * 16, count), jnp.float32),
            pltpu.VMEM(winds.shape, jnp.float32),
            pltpu.VMEM(surface.shape, jnp.float32),
            pltpu.VMEM(turned.shape, jnp.float32),
            pltpu.SemaphoreType.DMA((levels + 1, 9)),
        ],
        compiler_params=LIMIT,
    )(live_count, neighbours, rotations, sums, held, ghosts, remote, inside_in, outside_in)
    return winds_out, surface_out, jnp.transpose(moved, (0, 1, 3, 2))


def solution(mesh):
    in_specs = (
        P(None, "lev", None, "elem"),
        P(None, "elem"),
        P("lev"),
        P("lev", None, "elem", None),
        P(None, "elem"),
        P(None, "elem"),
        P("elem"),
    )
    out_specs = (P(None, "lev", None, "elem"), P(None, "elem"), P("lev", None, "elem", None))
    return jax.shard_map(body, mesh=mesh, in_specs=in_specs, out_specs=out_specs, check_vma=False)
```

```python
import functools
import jax
import jax.numpy as jnp
import numpy as np
from jax import lax
from jax.experimental import pallas as pl
from jax.experimental.pallas import tpu as pltpu
from jax.sharding import PartitionSpec as P

STEP = 0.1
COURANT = 0.45
HALO = 16
NODE_EDGES = [[0, 1, 2, 3], [3, 7, 11, 15], [15, 14, 13, 12], [12, 8, 4, 0]]
NODE_RING = [0, 1, 2, 3, 7, 11, 15, 14, 13, 12, 8, 4]
CELL_RING = [0, 1, 2, 5, 8, 7, 6, 3]
FIELDS = 8


def tables():
    points = np.array([-1.0, -(0.2**0.5), 0.2**0.5, 1.0])
    products = np.array(
        [np.prod([points[a] - points[k] for k in range(4) if k != a]) for a in range(4)]
    )
    derivative = np.zeros((4, 4))
    for source in range(4):
        for target in range(4):
            if source != target:
                derivative[source, target] = (
                    products[source] / products[target] / (points[source] - points[target])
                )
        derivative[source, source] = sum(
            (1.0 / (points[source] - points[k]) for k in range(4) if k != source)
        )
    identity = np.eye(4)
    along_x = np.kron(identity, derivative)
    along_y = np.kron(derivative, identity)
    centers = np.array([-2.0 / 3.0, 0.0, 2.0 / 3.0])
    lagrange = np.array(
        [
            [
                np.prod([(t - points[k]) / (points[b] - points[k]) for k in range(4) if k != b])
                for b in range(4)
            ]
            for t in centers
        ]
    )
    return along_x.astype(np.float32), along_y.astype(np.float32), lagrange


def multiplicity(node):
    return 1 + sum(node in edge for edge in NODE_EDGES)


def exact_dot(a, b):
    return jnp.dot(a, b, precision=lax.Precision.HIGHEST, preferred_element_type=jnp.float32)


def column_kernel(thickness_in, matrix_in, winds_in, part, thickness, matrix, winds, sems):
    copies = [
        pltpu.make_async_copy(source, target, sems.at[number])
        for number, (source, target) in enumerate(
            ((winds_in, winds), (matrix_in, matrix), (thickness_in, thickness))
        )
    ]
    for copy in copies:
        copy.start()
    for copy in copies:
        copy.wait()
    levels = winds.shape[1]
    sums = []
    for component in range(2):
        total = thickness[0] * winds[component, 0]
        for level in range(1, levels):
            total = total + thickness[level] * winds[component, level]
        sums.append(total)
    part[...] = exact_dot(matrix[...], jnp.concatenate(sums, axis=0))


def first_of(ref):
    return ref[...][0]


def strips(live):
    even = lax.rem(lax.axis_index("elem"), 2) == 0
    start = first_of(live) - HALO
    tile = start // 128
    lane = start % 128
    return (
        (jnp.where(even, tile, 0), jnp.where(even, lane, 0)),
        (jnp.where(even, 0, tile), jnp.where(even, 0, lane)),
    )


def picks(line, wanted):
    return jnp.where(line == wanted, 1.0, 0.0).astype(jnp.bfloat16)


def split(values):
    high = values.astype(jnp.bfloat16)
    low = (values - high.astype(jnp.float32)).astype(jnp.bfloat16)
    return jnp.concatenate([high, low], axis=1)


def strip_kernel(live, tracers, order, held, border, inside, outside, sems):
    del order
    levels, _, tracer_total, count = tracers.shape
    loads = [
        pltpu.make_async_copy(tracers.at[level], held.at[level], sems.at[level])
        for level in range(levels)
    ]
    for load in loads:
        load.start()
    line = lax.broadcasted_iota(jnp.int32, (count, 256), 0)
    lane = lax.broadcasted_iota(jnp.int32, (count, 256), 1)
    starts = [128 * tile + at for tile, at in strips(live)]
    picker = picks(line, jnp.where(lane < 128, starts[0], starts[1]) + lane % HALO)
    picker = jnp.concatenate([picker, picker], axis=0)
    part = (lax.broadcasted_iota(jnp.int32, (BLOCK, 256), 1) % 128) // HALO
    for level in range(levels):
        loads[level].wait()
        for block in range(tracer_total // BLOCK):
            rows = pl.ds(BLOCK * block, BLOCK)
            for place, cell in enumerate(CELL_RING):
                border[level, block, pl.ds(BLOCK * place, BLOCK), :] = split(held[level, cell, rows, :])
            found = jnp.dot(border[level, block], picker, preferred_element_type=jnp.float32)
            packed = found[:BLOCK]
            for place in range(1, 8):
                packed = jnp.where(part == place, found[BLOCK * place : BLOCK * (place + 1)], packed)
            rows = pl.ds(level * tracer_total + BLOCK * block, BLOCK)
            inside[rows, :] = packed[:, :128]
            outside[rows, :] = packed[:, 128:]


def star_kernel(live, matrix, *refs):
    *parts, surface, winds, neighbours, rotations, border, inside_in, outside_in = refs[:-4]
    star, inside, outside, ghosts = refs[-4:]
    del inside_in, outside_in
    levels = winds.shape[1]
    column = parts[0][...]
    for part in parts[1:]:
        column = column + part[...]
    surface_star = surface[...] - STEP * column
    gradient = exact_dot(matrix[...], surface_star)
    for tile in range(2):
        lanes = slice(128 * tile, 128 * tile + 128)
        for component in range(2):
            slope = gradient[16 * component : 16 * component + 16, lanes]
            for level in range(levels):
                star[tile, pl.ds(levels * component + level, 16, stride=FIELDS), :] = (
                    winds[component, level, :, lanes] - STEP * slope
                )
        for field in range(2 * levels, FIELDS):
            star[tile, pl.ds(field, 16, stride=FIELDS), :] = surface_star[:, lanes]
    lane_block = lax.broadcasted_iota(jnp.int32, (FIELDS, 128), 1) // HALO
    base = inside.shape[0] - 2 * FIELDS
    for target, (tile, at) in zip((inside, outside), strips(live)):
        for block in range(2):
            packed = None
            for place in range(min(8, 12 - 8 * block)):
                node = NODE_RING[8 * block + place]
                values = star[tile, pl.ds(FIELDS * node, FIELDS), :]
                moved = pltpu.roll(values, lax.rem(HALO * place + 128 - at, 128), 1)
                packed = moved if packed is None else jnp.where(lane_block == place, moved, packed)
            target[pl.ds(base + FIELDS * block, FIELDS), :] = packed

    me = lax.axis_index("elem")

    @pl.when(me == 0)
    def _():
        near_ghosts(neighbours, rotations, border, ghosts, range(1))

    @pl.when(me == 1)
    def _():
        near_ghosts(neighbours, rotations, border, ghosts, range(levels))


def add_edges(nodes, codes, ring):
    for edge in range(4):
        code = codes[edge]
        found = ring(edge)
        for place in range(4):
            value = found((3 - place) % 12)
            for other in range(1, 4):
                value = jnp.where(code == other, found((3 * other + 3 - place) % 12), value)
            node = NODE_EDGES[edge][place]
            nodes[node] = nodes[node] + value


def rows_of(ref, edge, tile):
    return jnp.broadcast_to(ref[pl.ds(edge, 1), pl.ds(128 * tile, 128)], (FIELDS, 128))


def lane_gather(values, index):
    return jnp.take_along_axis(values, index, axis=1, mode="promise_in_bounds")


def weights(nodes, live, tile, factors):
    lagrange = tables()[2]
    rows = [
        [
            sum(float(lagrange[x, n]) * nodes[4 * y + n] for n in range(4))
            for x in range(3)
        ]
        for y in range(4)
    ]
    lanes = pl.ds(128 * tile, 128)
    lane = lax.broadcasted_iota(jnp.int32, (FIELDS, 128), 1) + 128 * tile
    row = lax.broadcasted_iota(jnp.int32, (FIELDS, 128), 0)
    alive = lane < live
    for y in range(3):
        for x in range(3):
            value = sum(float(lagrange[y, n]) * rows[n][x] for n in range(4))
            shift = COURANT * jnp.tanh(value)
            square = shift * shift
            low = 0.5 * (square + shift)
            high = 0.5 * (square - shift)
            middle = 1.0 - square - pltpu.roll(square, 6, 0)
            sides = jnp.where(row < 4, low, pltpu.roll(high, 4, 0))
            at = 16 * (3 * y + x)
            factors[pl.ds(at, 8), lanes] = jnp.where(alive, sides, 0.0)
            factors[pl.ds(at + 8, 8), lanes] = jnp.where(alive, middle, 0.0)


def near_ghosts(neighbours, rotations, border, ghosts, which):
    count = ghosts.shape[3]
    me = lax.axis_index("elem")
    line = lax.broadcasted_iota(jnp.int32, (count, count), 0)
    slots = neighbours[...]
    codes = rotations[...] & 3
    near = jnp.where(slots // count == me, slots % count, -1)
    pickers = []
    for edge in range(4):
        picker = picks(line, near[edge : edge + 1])
        pickers.append(jnp.concatenate([picker, picker], axis=0))
    chosen = [
        [jnp.broadcast_to(codes[edge : edge + 1] == other, (8, count)) for other in range(4)]
        for edge in range(4)
    ]
    for level in which:
        for block in range(border.shape[1]):
            for edge in range(4):
                ring = jnp.dot(border[level, block], pickers[edge], preferred_element_type=jnp.float32)
                for at in range(0, BLOCK, 8):
                    for place in range(3):
                        value = None
                        for other in range(4):
                            base = BLOCK * ((2 * other + 2 - place) % 8) + at
                            found = ring[base : base + 8]
                            value = found if value is None else jnp.where(chosen[edge][other], found, value)
                        ghosts[level, 3 * edge + place, pl.ds(BLOCK * block + at, 8), :] = value


def inner_kernel(neighbours, rotations, star, border, begun, order, sums, ghosts, remote):
    del begun, order
    levels, _, tracer_total, count = ghosts.shape
    me = lax.axis_index("elem")
    for tile in range(2):
        nodes = [star[tile, pl.ds(FIELDS * n, FIELDS), :] for n in range(16)]
        codes = [rows_of(rotations, edge, tile) & 3 for edge in range(4)]

        def ring(edge, tile=tile):
            slots = rows_of(neighbours, edge, tile)
            own = slots // count == me
            local = slots % count
            within = local % 128
            upper = local >= 128
            kept = {}

            def found(place):
                if place not in kept:
                    at = pl.ds(FIELDS * NODE_RING[place], FIELDS)
                    both = jnp.where(
                        upper, lane_gather(star[1, at, :], within), lane_gather(star[0, at, :], within)
                    )
                    kept[place] = jnp.where(own, both, 0.0)
                return kept[place]

            return found

        add_edges(nodes, codes, ring)
        for n in range(16):
            sums[tile, pl.ds(FIELDS * n, FIELDS), :] = nodes[n]

    devices = lax.axis_size("elem")
    line = lax.broadcasted_iota(jnp.int32, (count, count), 0)
    slots = neighbours[...]
    own = slots // count == me
    after = slots // count == lax.rem(me + 1, devices)
    codes = rotations[...] & 3
    for place in range(3):
        source = HALO * ((2 * codes + 2 - place) & 7) + slots % HALO + jnp.where(after, 128, 0)
        source = jnp.where(own, -1, source)
        for edge in range(4):
            remote[3 * edge + place] = picks(line, source[edge : edge + 1])

    @pl.when(me > 1)
    def _():
        near_ghosts(neighbours, rotations, border, ghosts, range(1))

    @pl.when(me != 1)
    def _():
        near_ghosts(neighbours, rotations, border, ghosts, range(1, levels))


def outer_kernel(
    live,
    neighbours,
    rotations,
    sums,
    held,
    near,
    remote,
    outside,
    inside,
    winds_out,
    surface_out,
    moved,
    means,
    factors,
    winds_new,
    surface_new,
    done,
    sems,
):
    levels, _, tracer_total, count = held.shape
    me = lax.axis_index("elem")
    devices = lax.axis_size("elem")
    even = lax.rem(me, 2) == 0
    alive = first_of(live)
    base = levels * tracer_total

    def both_sides(rows):
        left, right = inside[rows, :], outside[rows, :]
        return jnp.where(even, right, left), jnp.where(even, left, right)

    node_halo = [both_sides(pl.ds(base + FIELDS * block, FIELDS)) for block in range(2)]
    for tile in range(2):
        nodes = [sums[tile, pl.ds(FIELDS * n, FIELDS), :] for n in range(16)]
        for edge in range(4):
            slots = rows_of(neighbours, edge, tile)
            code = rows_of(rotations, edge, tile) & 3
            owner = slots // count
            other = owner != me
            after = owner == lax.rem(me + 1, devices)
            for place in range(4):
                spot = 3 * code + 3 - place
                spot = jnp.where(spot >= 12, spot - 12, spot)
                index = HALO * (spot & 7) + (slots & (HALO - 1))
                high = spot >= 8
                value = jnp.where(
                    high, lane_gather(node_halo[1][1], index), lane_gather(node_halo[0][1], index)
                )
                if tile == 0:
                    behind = jnp.where(
                        high, lane_gather(node_halo[1][0], index), lane_gather(node_halo[0][0], index)
                    )
                    value = jnp.where(after, value, behind)
                node = NODE_EDGES[edge][place]
                nodes[node] = nodes[node] + jnp.where(other, value, 0.0)
        nodes = [nodes[n] * (1.0 / multiplicity(n)) for n in range(16)]
        weights(nodes, alive, tile, factors)
        lane = lax.broadcasted_iota(jnp.int32, (FIELDS, 128), 1) + 128 * tile
        for n in range(16):
            means[tile, pl.ds(FIELDS * n, FIELDS), :] = jnp.where(lane < alive, nodes[n], 0.0)
        lanes = pl.ds(128 * tile, 128)
        for component in range(2):
            for level in range(levels):
                winds_new[component, level, :, lanes] = means[
                    tile, pl.ds(levels * component + level, 16, stride=FIELDS), :
                ]
        surface_new[:, lanes] = means[tile, pl.ds(2 * levels, 16, stride=FIELDS), :]

    copies = [
        pltpu.make_async_copy(winds_new, winds_out, sems.at[levels, 0]),
        pltpu.make_async_copy(surface_new, surface_out, sems.at[levels, 1]),
    ]
    for copy in copies:
        copy.start()

    strip = split(jnp.concatenate(both_sides(pl.ds(0, base)), axis=1))

    def ghost(edge, place):
        number = 3 * edge + place
        picker = remote[number]
        found = jnp.dot(
            strip, jnp.concatenate([picker, picker], axis=0), preferred_element_type=jnp.float32
        )
        return [
            near[level, number] + found[level * tracer_total : (level + 1) * tracer_total]
            for level in range(levels)
        ]

    def own(cell):
        return [held[level, cell] for level in range(levels)]

    for cell in CELL_ORDER:
        row, col = cell // 3, cell % 3
        west = own(cell - 1) if col > 0 else ghost(3, 2 - row)
        east = own(cell + 1) if col < 2 else ghost(1, row)
        south = own(cell - 3) if row > 0 else ghost(0, col)
        north = own(cell + 3) if row < 2 else ghost(2, 2 - col)
        for level in range(levels):
            factor = [factors[pl.ds(16 * cell + at + level, 1), :] for at in (0, 2, 4, 6, 8)]
            done[level, cell] = (
                held[level, cell] * factor[4]
                + (west[level] * factor[0] + east[level] * factor[2])
                + (south[level] * factor[1] + north[level] * factor[3])
            )
            copy = pltpu.make_async_copy(done.at[level, cell], moved.at[level, cell], sems.at[level, cell])
            copy.start()
            copies.append(copy)
    for copy in copies:
        copy.wait()


VMEM = pl.BlockSpec(memory_space=pltpu.VMEM)
SMEM = pl.BlockSpec(memory_space=pltpu.SMEM)
HBM = pl.BlockSpec(memory_space=pltpu.HBM)
ANY = pl.BlockSpec(memory_space=pl.ANY)
LIMIT = pltpu.CompilerParams(vmem_limit_bytes=20 * 1024 * 1024)
CELL_ORDER = [4, 1, 3, 5, 7, 0, 2, 6, 8]
BLOCK = 112


def in_hbm(array):
    return pltpu.with_memory_space_constraint(array, pltpu.HBM)


def body(winds, surface, thickness, tracers, neighbours, rotations, live_count):
    levels, _, count, tracer_total = tracers.shape
    along_x, along_y, _ = tables()
    across = jnp.asarray(np.concatenate([along_x, along_y], axis=1))
    down = jnp.asarray(np.concatenate([along_x, along_y], axis=0))
    f32 = functools.partial(jax.ShapeDtypeStruct, dtype=jnp.float32)
    turned = jnp.transpose(tracers, (0, 1, 3, 2))
    pack_shape = (levels * tracer_total + 2 * FIELDS, 128)

    part = pl.pallas_call(
        column_kernel,
        name="column",
        in_specs=[HBM] * 3,
        out_specs=VMEM,
        out_shape=f32((16, count)),
        scratch_shapes=[
            pltpu.SMEM(thickness.shape, jnp.float32),
            pltpu.VMEM(across.shape, jnp.float32),
            pltpu.VMEM(winds.shape, jnp.float32),
            pltpu.SemaphoreType.DMA((3,)),
        ],
        compiler_params=LIMIT,
    )(in_hbm(thickness), in_hbm(across), in_hbm(winds))

    ranks = lax.axis_size("lev")
    parts = [part]
    for step in range(1, ranks):
        parts.append(lax.ppermute(part, "lev", [(i, i ^ step) for i in range(ranks)]))

    held, border, inside, outside = pl.pallas_call(
        strip_kernel,
        name="strips",
        in_specs=[VMEM, HBM, ANY],
        out_specs=[VMEM] * 4,
        out_shape=[
            pltpu.VMEM(turned.shape, jnp.float32),
            pltpu.VMEM((levels, tracer_total // BLOCK, 8 * BLOCK, 2 * count), jnp.bfloat16),
            pltpu.VMEM(pack_shape, jnp.float32),
            pltpu.VMEM(pack_shape, jnp.float32),
        ],
        scratch_shapes=[pltpu.SemaphoreType.DMA((levels,))],
        compiler_params=LIMIT,
    )(live_count, in_hbm(turned), part)

    ghosts_shape = pltpu.VMEM((levels, 12, tracer_total, count), jnp.float32)
    star, inside, outside, ghosts = pl.pallas_call(
        star_kernel,
        name="star",
        in_specs=[VMEM, VMEM] + [VMEM] * (ranks + 7),
        out_specs=[VMEM] * 4,
        out_shape=[
            pltpu.VMEM((2, 16 * FIELDS, 128), jnp.float32),
            pltpu.VMEM(pack_shape, jnp.float32),
            pltpu.VMEM(pack_shape, jnp.float32),
            ghosts_shape,
        ],
        input_output_aliases={ranks + 7: 1, ranks + 8: 2},
        compiler_params=LIMIT,
    )(live_count, down, *parts, surface, winds, neighbours, rotations, border, inside, outside)

    devices = lax.axis_size("elem")
    outside_in = lax.ppermute(
        outside, "elem", [(i, (((i + 1) % devices ^ 1) - 1) % devices) for i in range(devices)]
    )
    inside_in = lax.ppermute(inside, "elem", [(i, i ^ 1) for i in range(devices)])

    sums, ghosts, remote = pl.pallas_call(
        inner_kernel,
        name="inner",
        in_specs=[VMEM] * 5 + [ANY],
        input_output_aliases={4: 1},
        out_specs=[VMEM, VMEM, VMEM],
        out_shape=[
            pltpu.VMEM((2, 16 * FIELDS, 128), jnp.float32),
            ghosts_shape,
            pltpu.VMEM((12, count, count), jnp.bfloat16),
        ],
        compiler_params=LIMIT,
    )(neighbours, rotations, star, border, ghosts, star)

    winds_out, surface_out, moved = pl.pallas_call(
        outer_kernel,
        name="outer",
        in_specs=[VMEM] + [VMEM] * 8,
        out_specs=[HBM] * 3,
        out_shape=[f32(winds.shape), f32(surface.shape), f32(turned.shape)],
        scratch_shapes=[
            pltpu.VMEM((2, 16 * FIELDS, 128), jnp.float32),
            pltpu.VMEM((9 * 16, count), jnp.float32),
            pltpu.VMEM(winds.shape, jnp.float32),
            pltpu.VMEM(surface.shape, jnp.float32),
            pltpu.VMEM(turned.shape, jnp.float32),
            pltpu.SemaphoreType.DMA((levels + 1, 9)),
        ],
        compiler_params=LIMIT,
    )(live_count, neighbours, rotations, sums, held, ghosts, remote, outside_in, inside_in)
    return winds_out, surface_out, jnp.transpose(moved, (0, 1, 3, 2))


def solution(mesh):
    in_specs = (
        P(None, "lev", None, "elem"),
        P(None, "elem"),
        P("lev"),
        P("lev", None, "elem", None),
        P(None, "elem"),
        P(None, "elem"),
        P("elem"),
    )
    out_specs = (P(None, "lev", None, "elem"), P(None, "elem"), P("lev", None, "elem", None))
    return jax.shard_map(body, mesh=mesh, in_specs=in_specs, out_specs=out_specs, check_vma=False)
```

```python
import functools
import jax
import jax.numpy as jnp
import numpy as np
from jax import lax
from jax.experimental import pallas as pl
from jax.experimental.pallas import tpu as pltpu
from jax.sharding import PartitionSpec as P

STEP = 0.1
COURANT = 0.45
HALO = 16
NODE_EDGES = [[0, 1, 2, 3], [3, 7, 11, 15], [15, 14, 13, 12], [12, 8, 4, 0]]
NODE_RING = [0, 1, 2, 3, 7, 11, 15, 14, 13, 12, 8, 4]
CELL_RING = [0, 1, 2, 5, 8, 7, 6, 3]
FIELDS = 8


def tables():
    points = np.array([-1.0, -(0.2**0.5), 0.2**0.5, 1.0])
    products = np.array(
        [np.prod([points[a] - points[k] for k in range(4) if k != a]) for a in range(4)]
    )
    derivative = np.zeros((4, 4))
    for source in range(4):
        for target in range(4):
            if source != target:
                derivative[source, target] = (
                    products[source] / products[target] / (points[source] - points[target])
                )
        derivative[source, source] = sum(
            (1.0 / (points[source] - points[k]) for k in range(4) if k != source)
        )
    identity = np.eye(4)
    along_x = np.kron(identity, derivative)
    along_y = np.kron(derivative, identity)
    centers = np.array([-2.0 / 3.0, 0.0, 2.0 / 3.0])
    lagrange = np.array(
        [
            [
                np.prod([(t - points[k]) / (points[b] - points[k]) for k in range(4) if k != b])
                for b in range(4)
            ]
            for t in centers
        ]
    )
    return along_x.astype(np.float32), along_y.astype(np.float32), lagrange


def multiplicity(node):
    return 1 + sum(node in edge for edge in NODE_EDGES)


def exact_dot(a, b):
    return jnp.dot(a, b, precision=lax.Precision.HIGHEST, preferred_element_type=jnp.float32)


def column_kernel(thickness_in, matrix_in, winds_in, part, thickness, matrix, winds, sems):
    copies = [
        pltpu.make_async_copy(source, target, sems.at[number])
        for number, (source, target) in enumerate(
            ((winds_in, winds), (matrix_in, matrix), (thickness_in, thickness))
        )
    ]
    for copy in copies:
        copy.start()
    for copy in copies:
        copy.wait()
    levels = winds.shape[1]
    sums = []
    for component in range(2):
        total = thickness[0] * winds[component, 0]
        for level in range(1, levels):
            total = total + thickness[level] * winds[component, level]
        sums.append(total)
    part[...] = exact_dot(matrix[...], jnp.concatenate(sums, axis=0))


def first_of(ref):
    return ref[...][0]


def strips(live):
    even = lax.rem(lax.axis_index("elem"), 2) == 0
    start = first_of(live) - HALO
    tile = start // 128
    lane = start % 128
    return (
        (jnp.where(even, tile, 0), jnp.where(even, lane, 0)),
        (jnp.where(even, 0, tile), jnp.where(even, 0, lane)),
    )


def picks(line, wanted):
    return jnp.where(line == wanted, 1.0, 0.0).astype(jnp.bfloat16)


def split(values):
    high = values.astype(jnp.bfloat16)
    low = (values - high.astype(jnp.float32)).astype(jnp.bfloat16)
    return jnp.concatenate([high, low], axis=1)


def strip_kernel(live, tracers, order, held, border, inside, outside, sems):
    del order
    levels, _, tracer_total, count = tracers.shape
    loads = {}
    for level in range(levels):
        for block in range(tracer_total // BLOCK):
            where = (level, slice(None), pl.ds(BLOCK * block, BLOCK))
            loads[level, block] = pltpu.make_async_copy(
                tracers.at[where], held.at[where], sems.at[level, block]
            )
            loads[level, block].start()
    line = lax.broadcasted_iota(jnp.int32, (count, 256), 0)
    lane = lax.broadcasted_iota(jnp.int32, (count, 256), 1)
    starts = [128 * tile + at for tile, at in strips(live)]
    picker = picks(line, jnp.where(lane < 128, starts[0], starts[1]) + lane % HALO)
    picker = jnp.concatenate([picker, picker], axis=0)
    part = (lax.broadcasted_iota(jnp.int32, (BLOCK, 256), 1) % 128) // HALO
    for level in range(levels):
        for block in range(tracer_total // BLOCK):
            loads[level, block].wait()
            rows = pl.ds(BLOCK * block, BLOCK)
            for place, cell in enumerate(CELL_RING):
                border[level, block, pl.ds(BLOCK * place, BLOCK), :] = split(held[level, cell, rows, :])
            found = jnp.dot(border[level, block], picker, preferred_element_type=jnp.float32)
            packed = found[:BLOCK]
            for place in range(1, 8):
                packed = jnp.where(part == place, found[BLOCK * place : BLOCK * (place + 1)], packed)
            rows = pl.ds(level * tracer_total + BLOCK * block, BLOCK)
            inside[rows, :] = packed[:, :128]
            outside[rows, :] = packed[:, 128:]


def star_kernel(live, matrix, *refs):
    *parts, surface, winds, neighbours, rotations, border, inside_in, outside_in = refs[:-4]
    star, inside, outside, ghosts = refs[-4:]
    del inside_in, outside_in
    levels = winds.shape[1]
    column = parts[0][...]
    for part in parts[1:]:
        column = column + part[...]
    surface_star = surface[...] - STEP * column
    gradient = exact_dot(matrix[...], surface_star)
    for tile in range(2):
        lanes = slice(128 * tile, 128 * tile + 128)
        for component in range(2):
            slope = gradient[16 * component : 16 * component + 16, lanes]
            for level in range(levels):
                star[tile, pl.ds(levels * component + level, 16, stride=FIELDS), :] = (
                    winds[component, level, :, lanes] - STEP * slope
                )
        for field in range(2 * levels, FIELDS):
            star[tile, pl.ds(field, 16, stride=FIELDS), :] = surface_star[:, lanes]
    lane_block = lax.broadcasted_iota(jnp.int32, (FIELDS, 128), 1) // HALO
    base = inside.shape[0] - 2 * FIELDS
    for target, (tile, at) in zip((inside, outside), strips(live)):
        for block in range(2):
            packed = None
            for place in range(min(8, 12 - 8 * block)):
                node = NODE_RING[8 * block + place]
                values = star[tile, pl.ds(FIELDS * node, FIELDS), :]
                moved = pltpu.roll(values, lax.rem(HALO * place + 128 - at, 128), 1)
                packed = moved if packed is None else jnp.where(lane_block == place, moved, packed)
            target[pl.ds(base + FIELDS * block, FIELDS), :] = packed

    me = lax.axis_index("elem")

    @pl.when(me == 0)
    def _():
        near_ghosts(neighbours, rotations, border, ghosts, range(1))

    @pl.when(me == 1)
    def _():
        near_ghosts(neighbours, rotations, border, ghosts, range(levels))


def add_edges(nodes, codes, ring):
    for edge in range(4):
        code = codes[edge]
        found = ring(edge)
        for place in range(4):
            value = found((3 - place) % 12)
            for other in range(1, 4):
                value = jnp.where(code == other, found((3 * other + 3 - place) % 12), value)
            node = NODE_EDGES[edge][place]
            nodes[node] = nodes[node] + value


def rows_of(ref, edge, tile):
    return jnp.broadcast_to(ref[pl.ds(edge, 1), pl.ds(128 * tile, 128)], (FIELDS, 128))


def lane_gather(values, index):
    return jnp.take_along_axis(values, index, axis=1, mode="promise_in_bounds")


def weights(nodes, live, tile, factors):
    lagrange = tables()[2]
    rows = [
        [
            sum(float(lagrange[x, n]) * nodes[4 * y + n] for n in range(4))
            for x in range(3)
        ]
        for y in range(4)
    ]
    lanes = pl.ds(128 * tile, 128)
    lane = lax.broadcasted_iota(jnp.int32, (FIELDS, 128), 1) + 128 * tile
    row = lax.broadcasted_iota(jnp.int32, (FIELDS, 128), 0)
    alive = lane < live
    for y in range(3):
        for x in range(3):
            value = sum(float(lagrange[y, n]) * rows[n][x] for n in range(4))
            shift = COURANT * jnp.tanh(value)
            square = shift * shift
            low = 0.5 * (square + shift)
            high = 0.5 * (square - shift)
            middle = 1.0 - square - pltpu.roll(square, 6, 0)
            sides = jnp.where(row < 4, low, pltpu.roll(high, 4, 0))
            at = 16 * (3 * y + x)
            factors[pl.ds(at, 8), lanes] = jnp.where(alive, sides, 0.0)
            factors[pl.ds(at + 8, 8), lanes] = jnp.where(alive, middle, 0.0)


def near_ghosts(neighbours, rotations, border, ghosts, which):
    count = ghosts.shape[3]
    me = lax.axis_index("elem")
    line = lax.broadcasted_iota(jnp.int32, (count, count), 0)
    slots = neighbours[...]
    codes = rotations[...] & 3
    near = jnp.where(slots // count == me, slots % count, -1)
    pickers = []
    for edge in range(4):
        picker = picks(line, near[edge : edge + 1])
        pickers.append(jnp.concatenate([picker, picker], axis=0))
    chosen = [
        [jnp.broadcast_to(codes[edge : edge + 1] == other, (8, count)) for other in range(4)]
        for edge in range(4)
    ]
    for level in which:
        for block in range(border.shape[1]):
            for edge in range(4):
                ring = jnp.dot(border[level, block], pickers[edge], preferred_element_type=jnp.float32)
                for at in range(0, BLOCK, 8):
                    for place in range(3):
                        value = None
                        for other in range(4):
                            base = BLOCK * ((2 * other + 2 - place) % 8) + at
                            found = ring[base : base + 8]
                            value = found if value is None else jnp.where(chosen[edge][other], found, value)
                        ghosts[level, 3 * edge + place, pl.ds(BLOCK * block + at, 8), :] = value


def inner_kernel(neighbours, rotations, star, border, begun, order, sums, ghosts, remote):
    del begun, order
    levels, _, tracer_total, count = ghosts.shape
    me = lax.axis_index("elem")
    for tile in range(2):
        nodes = [star[tile, pl.ds(FIELDS * n, FIELDS), :] for n in range(16)]
        codes = [rows_of(rotations, edge, tile) & 3 for edge in range(4)]

        def ring(edge, tile=tile):
            slots = rows_of(neighbours, edge, tile)
            own = slots // count == me
            local = slots % count
            within = local % 128
            upper = local >= 128
            kept = {}

            def found(place):
                if place not in kept:
                    at = pl.ds(FIELDS * NODE_RING[place], FIELDS)
                    both = jnp.where(
                        upper, lane_gather(star[1, at, :], within), lane_gather(star[0, at, :], within)
                    )
                    kept[place] = jnp.where(own, both, 0.0)
                return kept[place]

            return found

        add_edges(nodes, codes, ring)
        for n in range(16):
            sums[tile, pl.ds(FIELDS * n, FIELDS), :] = nodes[n]

    devices = lax.axis_size("elem")
    line = lax.broadcasted_iota(jnp.int32, (count, count), 0)
    slots = neighbours[...]
    own = slots // count == me
    after = slots // count == lax.rem(me + 1, devices)
    codes = rotations[...] & 3
    for place in range(3):
        source = HALO * ((2 * codes + 2 - place) & 7) + slots % HALO + jnp.where(after, 128, 0)
        source = jnp.where(own, -1, source)
        for edge in range(4):
            remote[3 * edge + place] = picks(line, source[edge : edge + 1])

    @pl.when(me > 1)
    def _():
        near_ghosts(neighbours, rotations, border, ghosts, range(1))

    @pl.when(me != 1)
    def _():
        near_ghosts(neighbours, rotations, border, ghosts, range(1, levels))


def outer_kernel(
    live,
    neighbours,
    rotations,
    sums,
    held,
    near,
    remote,
    outside,
    inside,
    winds_out,
    surface_out,
    moved,
    means,
    factors,
    winds_new,
    surface_new,
    done,
    sems,
):
    levels, _, tracer_total, count = held.shape
    me = lax.axis_index("elem")
    devices = lax.axis_size("elem")
    even = lax.rem(me, 2) == 0
    alive = first_of(live)
    base = levels * tracer_total

    def both_sides(rows):
        left, right = inside[rows, :], outside[rows, :]
        return jnp.where(even, right, left), jnp.where(even, left, right)

    node_halo = [both_sides(pl.ds(base + FIELDS * block, FIELDS)) for block in range(2)]
    for tile in range(2):
        nodes = [sums[tile, pl.ds(FIELDS * n, FIELDS), :] for n in range(16)]
        for edge in range(4):
            slots = rows_of(neighbours, edge, tile)
            code = rows_of(rotations, edge, tile) & 3
            owner = slots // count
            other = owner != me
            after = owner == lax.rem(me + 1, devices)
            for place in range(4):
                spot = 3 * code + 3 - place
                spot = jnp.where(spot >= 12, spot - 12, spot)
                index = HALO * (spot & 7) + (slots & (HALO - 1))
                high = spot >= 8
                value = jnp.where(
                    high, lane_gather(node_halo[1][1], index), lane_gather(node_halo[0][1], index)
                )
                if tile == 0:
                    behind = jnp.where(
                        high, lane_gather(node_halo[1][0], index), lane_gather(node_halo[0][0], index)
                    )
                    value = jnp.where(after, value, behind)
                node = NODE_EDGES[edge][place]
                nodes[node] = nodes[node] + jnp.where(other, value, 0.0)
        nodes = [nodes[n] * (1.0 / multiplicity(n)) for n in range(16)]
        weights(nodes, alive, tile, factors)
        lane = lax.broadcasted_iota(jnp.int32, (FIELDS, 128), 1) + 128 * tile
        for n in range(16):
            means[tile, pl.ds(FIELDS * n, FIELDS), :] = jnp.where(lane < alive, nodes[n], 0.0)
        lanes = pl.ds(128 * tile, 128)
        for component in range(2):
            for level in range(levels):
                winds_new[component, level, :, lanes] = means[
                    tile, pl.ds(levels * component + level, 16, stride=FIELDS), :
                ]
        surface_new[:, lanes] = means[tile, pl.ds(2 * levels, 16, stride=FIELDS), :]

    copies = [
        pltpu.make_async_copy(winds_new, winds_out, sems.at[levels, 0]),
        pltpu.make_async_copy(surface_new, surface_out, sems.at[levels, 1]),
    ]
    for copy in copies:
        copy.start()

    strip = split(jnp.concatenate(both_sides(pl.ds(0, base)), axis=1))

    def ghost(edge, place):
        number = 3 * edge + place
        picker = remote[number]
        found = jnp.dot(
            strip, jnp.concatenate([picker, picker], axis=0), preferred_element_type=jnp.float32
        )
        return [
            near[level, number] + found[level * tracer_total : (level + 1) * tracer_total]
            for level in range(levels)
        ]

    def own(cell):
        return [held[level, cell] for level in range(levels)]

    for cell in CELL_ORDER:
        row, col = cell // 3, cell % 3
        west = own(cell - 1) if col > 0 else ghost(3, 2 - row)
        east = own(cell + 1) if col < 2 else ghost(1, row)
        south = own(cell - 3) if row > 0 else ghost(0, col)
        north = own(cell + 3) if row < 2 else ghost(2, 2 - col)
        for level in range(levels):
            factor = [factors[pl.ds(16 * cell + at + level, 1), :] for at in (0, 2, 4, 6, 8)]
            done[level, cell] = (
                held[level, cell] * factor[4]
                + (west[level] * factor[0] + east[level] * factor[2])
                + (south[level] * factor[1] + north[level] * factor[3])
            )
            copy = pltpu.make_async_copy(done.at[level, cell], moved.at[level, cell], sems.at[level, cell])
            copy.start()
            copies.append(copy)
    for copy in copies:
        copy.wait()


VMEM = pl.BlockSpec(memory_space=pltpu.VMEM)
SMEM = pl.BlockSpec(memory_space=pltpu.SMEM)
HBM = pl.BlockSpec(memory_space=pltpu.HBM)
ANY = pl.BlockSpec(memory_space=pl.ANY)
LIMIT = pltpu.CompilerParams(vmem_limit_bytes=20 * 1024 * 1024)
CELL_ORDER = [4, 1, 3, 5, 7, 0, 2, 6, 8]
BLOCK = 112


def in_hbm(array):
    return pltpu.with_memory_space_constraint(array, pltpu.HBM)


def body(winds, surface, thickness, tracers, neighbours, rotations, live_count):
    levels, _, count, tracer_total = tracers.shape
    along_x, along_y, _ = tables()
    across = jnp.asarray(np.concatenate([along_x, along_y], axis=1))
    down = jnp.asarray(np.concatenate([along_x, along_y], axis=0))
    f32 = functools.partial(jax.ShapeDtypeStruct, dtype=jnp.float32)
    turned = jnp.transpose(tracers, (0, 1, 3, 2))
    pack_shape = (levels * tracer_total + 2 * FIELDS, 128)

    part = pl.pallas_call(
        column_kernel,
        name="column",
        in_specs=[HBM] * 3,
        out_specs=VMEM,
        out_shape=f32((16, count)),
        scratch_shapes=[
            pltpu.SMEM(thickness.shape, jnp.float32),
            pltpu.VMEM(across.shape, jnp.float32),
            pltpu.VMEM(winds.shape, jnp.float32),
            pltpu.SemaphoreType.DMA((3,)),
        ],
        compiler_params=LIMIT,
    )(in_hbm(thickness), in_hbm(across), in_hbm(winds))

    ranks = lax.axis_size("lev")
    parts = [part]
    for step in range(1, ranks):
        parts.append(lax.ppermute(part, "lev", [(i, i ^ step) for i in range(ranks)]))

    held, border, inside, outside = pl.pallas_call(
        strip_kernel,
        name="strips",
        in_specs=[VMEM, HBM, ANY],
        out_specs=[VMEM] * 4,
        out_shape=[
            pltpu.VMEM(turned.shape, jnp.float32),
            pltpu.VMEM((levels, tracer_total // BLOCK, 8 * BLOCK, 2 * count), jnp.bfloat16),
            pltpu.VMEM(pack_shape, jnp.float32),
            pltpu.VMEM(pack_shape, jnp.float32),
        ],
        scratch_shapes=[pltpu.SemaphoreType.DMA((levels, tracer_total // BLOCK))],
        compiler_params=LIMIT,
    )(live_count, in_hbm(turned), part)

    ghosts_shape = pltpu.VMEM((levels, 12, tracer_total, count), jnp.float32)
    star, inside, outside, ghosts = pl.pallas_call(
        star_kernel,
        name="star",
        in_specs=[VMEM, VMEM] + [VMEM] * (ranks + 7),
        out_specs=[VMEM] * 4,
        out_shape=[
            pltpu.VMEM((2, 16 * FIELDS, 128), jnp.float32),
            pltpu.VMEM(pack_shape, jnp.float32),
            pltpu.VMEM(pack_shape, jnp.float32),
            ghosts_shape,
        ],
        input_output_aliases={ranks + 7: 1, ranks + 8: 2},
        compiler_params=LIMIT,
    )(live_count, down, *parts, surface, winds, neighbours, rotations, border, inside, outside)

    devices = lax.axis_size("elem")
    outside_in = lax.ppermute(
        outside, "elem", [(i, (((i + 1) % devices ^ 1) - 1) % devices) for i in range(devices)]
    )
    inside_in = lax.ppermute(inside, "elem", [(i, i ^ 1) for i in range(devices)])

    sums, ghosts, remote = pl.pallas_call(
        inner_kernel,
        name="inner",
        in_specs=[VMEM] * 5 + [ANY],
        input_output_aliases={4: 1},
        out_specs=[VMEM, VMEM, VMEM],
        out_shape=[
            pltpu.VMEM((2, 16 * FIELDS, 128), jnp.float32),
            ghosts_shape,
            pltpu.VMEM((12, count, count), jnp.bfloat16),
        ],
        compiler_params=LIMIT,
    )(neighbours, rotations, star, border, ghosts, star)

    winds_out, surface_out, moved = pl.pallas_call(
        outer_kernel,
        name="outer",
        in_specs=[VMEM] + [VMEM] * 8,
        out_specs=[HBM] * 3,
        out_shape=[f32(winds.shape), f32(surface.shape), f32(turned.shape)],
        scratch_shapes=[
            pltpu.VMEM((2, 16 * FIELDS, 128), jnp.float32),
            pltpu.VMEM((9 * 16, count), jnp.float32),
            pltpu.VMEM(winds.shape, jnp.float32),
            pltpu.VMEM(surface.shape, jnp.float32),
            pltpu.VMEM(turned.shape, jnp.float32),
            pltpu.SemaphoreType.DMA((levels + 1, 9)),
        ],
        compiler_params=LIMIT,
    )(live_count, neighbours, rotations, sums, held, ghosts, remote, outside_in, inside_in)
    return winds_out, surface_out, jnp.transpose(moved, (0, 1, 3, 2))


def solution(mesh):
    in_specs = (
        P(None, "lev", None, "elem"),
        P(None, "elem"),
        P("lev"),
        P("lev", None, "elem", None),
        P(None, "elem"),
        P(None, "elem"),
        P("elem"),
    )
    out_specs = (P(None, "lev", None, "elem"), P(None, "elem"), P("lev", None, "elem", None))
    return jax.shard_map(body, mesh=mesh, in_specs=in_specs, out_specs=out_specs, check_vma=False)
```
